32 devices in a mesh: grp: 2 (over y), store: 4 (over z), tp: 4 (over x, core).
Axes of the slice: x: 2, y: 2, z: 4, core: 2. Of those that a mesh axis runs over, the one named last changes fastest.
Arguments:
- hidden: bfloat16 [512, 2, 8192], P(('grp', 'store'), None, 'tp'), parts along dimension 0, may hold values from -6 to 6
- queries: bfloat16 [512, 2, 8192], P(('grp', 'store'), None, 'tp'), parts along dimension 0, may hold values from -16 to 16
- fresh_rotated_keys: bfloat16 [512, 2, 1024], P(('grp', 'store'), None, 'tp'), parts along dimension 0, may hold values from -6 to 6
- value_matrix: bfloat16 [8192, 1024], P('tp'), may hold values from -0.0625 to 0.0625
- adapter_down_factors: bfloat16 [8, 8192, 64], P('store', 'tp'), may hold values from -0.0625 to 0.0625
- adapter_up_factors: bfloat16 [8, 64, 1024], P('store', None, 'tp'), may hold values from -0.375 to 0.375
- adapter_index_rows: int32 [512, 1], P(('grp', 'store')), parts along dimension 0, may hold values from 0 to 7; in each aligned block of 64 rows (0 to 63, 64 to 127, ...) at most 16 rows name the same one
- key_value_pool: bfloat16 [2, 128, 16, 1024], P(None, ('grp', 'store'), None, 'tp'), parts along dimension 1, may hold values from -6 to 6
- row_page_table: int32 [512, 64], P(('grp', 'store')), parts along dimension 0, may hold values from 0 to 15
- context_length: int32 [512], P(('grp', 'store')), parts along dimension 0, may hold values from 1 to 1024
- relocated_rows: int32 [128], P(('grp', 'store')), parts along dimension 0, may hold values from 0 to 63, as said below
- relocated_destination: int32 [128, 1], P(('grp', 'store')), parts along dimension 0, may hold values from 0 to 3; in each aligned block of 16 rows (0 to 15, 16 to 31, ...) at most 8 rows name the same one
Outputs:
- attention: bfloat16 [512, 2, 8192], P(('grp', 'store'), None, 'tp'), parts along dimension 0
- fresh_values: bfloat16 [512, 2, 1024], P(('grp', 'store'), None, 'tp'), parts along dimension 0
The draws below stay inside these ranges and needn't reach their ends.
There are 2 independent parts, one for each index of `grp`. The reference program is written for one: setup_inputs(seed, part) draws one part's arguments, and reference() takes and returns one part's arrays. A program takes and returns all parts, laid end to end along the dimension named above; an argument that names none is the same for every part. Nothing has to cross between parts.
Inputs may be any that keep to these rules, and one draw needn't show every extreme that they name: `adapter_index_rows`: in the rows of one store index no adapter is named by more than 16 rows, a bound that some block reaches. `relocated_destination`: among the 16 entries of one store index at most 8 name the same destination. `relocated_rows`: the 16 entries of one store index name distinct rows of that store index. `row_page_table`: entries index the pool of the row's holder.
All inputs are finite; a program needn't handle non-finite values.
Results may differ from the reference program's by a relative error of at most 0.014.
Values may be sent and summed in bfloat16 or wider, within the bound.
A program may use at most 128 MiB of HBM per device.

```python
import math
import jax
import jax.numpy as jnp
import numpy as np
from jax import lax

MODEL_WIDTH = 8192
HQ = 64
KEY_HEADS = 8
HEAD_WIDTH = 128
ADAPTER_RANK = 64
STEPS = 2
PAGE = 16
PAGES_ROW = 64
POOL = 16
ROW_DEV = 64
ROWS = 256
ADAPTER_TOTAL = 8
MOST = 16
MIG_DEV = 16
MIG_CAP = 8
MIGS = 64
CTX = 1024
POOLS = 64
N_STORE = 4


def draw_queries(key, part):
    key = jax.random.fold_in(key, 11)
    ques_raw = jax.random.truncated_normal(key, -6.0, 6.0, (ROWS, 2, HQ * HEAD_WIDTH), jnp.float32)
    return ques_raw.astype(jnp.bfloat16)


def draw_fresh_rotated_keys(key, part):
    key = jax.random.fold_in(key, 13)
    keys_raw = jax.random.truncated_normal(key, -6.0, 6.0, (ROWS, 2, KEY_HEADS * HEAD_WIDTH), jnp.float32)
    return keys_raw.astype(jnp.bfloat16)


def draw_context_length(key, part):
    key = jax.random.fold_in(key, 21)
    key_len, key_top, key_low = jax.random.split(key, 3)
    lengths = jax.random.randint(key_len, (ROWS,), 1, CTX + 1)
    longest = jax.random.randint(key_top, (), 0, ROWS)
    shortest = (longest + 1 + jax.random.randint(key_low, (), 0, ROWS - 1)) % ROWS
    lengths = lengths.at[longest].set(CTX).at[shortest].set(1)
    return lengths.astype(jnp.int32)


def draw_relocated_rows(key, part):
    key = jax.random.fold_in(key, 31)
    key_off, key_perm = jax.random.split(key, 2)
    blocks = MIGS // MIG_DEV
    stride = ROW_DEV // MIG_DEV
    offsets = jax.random.randint(key_off, (blocks, MIG_DEV), 0, stride)
    offsets = offsets.at[0, 0].set(0).at[0, MIG_DEV - 1].set(stride - 1)
    picks = jnp.arange(MIG_DEV, dtype=jnp.int32)[None, :] * stride + offsets
    orders = jax.vmap(lambda one_key: jax.random.permutation(one_key, MIG_DEV))(jax.random.split(key_perm, blocks))
    picks = jnp.take_along_axis(picks, orders, axis=1)
    return picks.reshape(MIGS).astype(jnp.int32)


def touch_ends(result, key, least, top_value):
    longest = result.shape.index(max(result.shape))
    spots = []
    for shift in (0, 1):
        where = [jax.random.randint(jax.random.fold_in(key, axis), (), 0, length) for axis, length in enumerate(result.shape)]
        where[longest] = (where[longest] + shift) % result.shape[longest]
        spots.append(tuple(where))
    return result.at[spots[0]].set(least).at[spots[1]].set(top_value)


def block_levels(key, dims, cuts, least, high):
    def one(position, shards_of):
        heights = jax.random.uniform(jax.random.fold_in(jax.random.fold_in(key, 6), position), (shards_of,), jnp.float32, least / len(cuts), high / len(cuts))
        return jnp.repeat(jnp.exp(heights), dims[position] // shards_of).reshape((-1,) + (1,) * (len(dims) - position - 1))

    loudness = one(*cuts[0])
    for cut in cuts[1:]:
        loudness = loudness * one(*cut)
    return loudness


def shared_out(rng, own, number, rows, count, top, most, skew):
    ranking = jax.random.permutation(rng, count)
    crowded, common = shares(count, rows * top, most, skew, True), shares(count, rows * top, most, skew, False)
    places = jnp.arange(count)

    def named(sizes, offset_by):
        used = int((sizes > 0).sum())
        fixed = max(1, used // 4)
        passed = fixed + (places - fixed + offset_by * (used - fixed)) % max(1, count - fixed)
        return jnp.zeros((count,), jnp.int32).at[ranking[jnp.where(places < fixed, places, passed)]].set(jnp.asarray(sizes, jnp.int32))

    sizes = jnp.where(number % 4 == 0, named(crowded, number // 4), named(common, number - number // 4 - 1))
    mixed = jax.random.permutation(jax.random.fold_in(own, 3), count)
    source_of, taker = mixed[0:count // 2 * 2:2], mixed[1:count // 2 * 2:2]
    slack = jnp.minimum(sizes[source_of] - 1, most - sizes[taker]) // 2
    slack = jnp.where((source_of == ranking[0]) | (taker == ranking[0]) | (sizes[taker] == 0), 0, jnp.maximum(slack, 0))
    passed = jax.random.randint(jax.random.fold_in(own, 4), (count // 2,), 0, 1 << 20) % (slack + 1)
    sizes = sizes.at[source_of].add(-passed).at[taker].add(passed)
    labels = jnp.searchsorted(jnp.cumsum(sizes), jnp.arange(rows * top), side="right").astype(jnp.int32)
    grid = labels.reshape(top, rows).T
    grid = grid[jax.random.permutation(jax.random.fold_in(own, 1), rows)]
    offset_by = jax.random.randint(jax.random.fold_in(own, 2), (rows, 1), 0, top)
    return jnp.take_along_axis(grid, (jnp.arange(top)[None, :] + offset_by) % top, axis=1)


def shares(count, total, most, lean, full):
    weights = [(1 << 20) // math.isqrt(standing ** lean) + 1 for standing in range(1, count + 1)]
    largest = most if full else min(most, max(-(-total // count), total * weights[0] // sum(weights)))
    least = 1 if total - largest >= count - 1 else 0
    holding, spare = [largest] + [least] * (count - 1), total - largest - least * (count - 1)
    while spare > 0:
        movable = [i for i in range(1, count) if holding[i] < largest] or [i for i in range(1, count) if holding[i] < most]
        pool, budget = sum([weights[i] for i in movable]), spare
        for i in movable:
            addition = min(most - holding[i], max(1, budget * weights[i] // pool), spare)
            holding[i] = holding[i] + addition
            spare = spare - addition
    return np.array(holding)


def scatter_about(own_key, extent, deviation, most, cuts=(), kind=jnp.bfloat16):
    result = deviation * jax.random.normal(own_key, extent, jnp.float32)
    if cuts:
        result = result * block_levels(own_key, extent, cuts, -0.22, 0.18)
    return jnp.clip(result, -most, most).astype(kind)


def setup_inputs(seed: int = 0, part: int = 0) -> dict:
    arg_keys = jax.random.split(jax.random.key(seed), 13)
    part_keys = jax.random.split(jax.random.fold_in(arg_keys[12], part), 13)
    hidden = scatter_about(part_keys[0], (ROWS, STEPS, MODEL_WIDTH), 1.0, 6.0, ((0, 4), (2, 4)))
    queries = draw_queries(jax.random.fold_in(jax.random.fold_in(arg_keys[12], part), 71), part)
    fresh_rotated_keys = draw_fresh_rotated_keys(jax.random.fold_in(jax.random.fold_in(arg_keys[12], part), 71), part)
    value_matrix = scatter_about(arg_keys[3], (MODEL_WIDTH, KEY_HEADS * HEAD_WIDTH), MODEL_WIDTH ** -0.5, 0.0625, ((0, 4),))
    adapter_down_factors = scatter_about(arg_keys[4], (ADAPTER_TOTAL, MODEL_WIDTH, ADAPTER_RANK), MODEL_WIDTH ** -0.5, 0.0625, ((0, 4), (1, 4)))
    adapter_up_factors = scatter_about(arg_keys[5], (ADAPTER_TOTAL, ADAPTER_RANK, KEY_HEADS * HEAD_WIDTH), (4 * ADAPTER_RANK) ** -0.5, 0.375, ((0, 4), (2, 4)))
    adapter_index_rows_keys = jax.random.split(jax.random.fold_in(part_keys[6], 1), ROWS // ROW_DEV)
    adapter_index_rows_turns = jax.random.permutation(jax.random.fold_in(part_keys[6], 3), ROWS // ROW_DEV)
    adapter_index_rows = jax.vmap(lambda own, number: shared_out(jax.random.fold_in(part_keys[6], 2), own, number, ROW_DEV, ADAPTER_TOTAL, 1, MOST, 2))(adapter_index_rows_keys, adapter_index_rows_turns).reshape((ROWS, 1))
    key_value_pool = scatter_about(part_keys[7], (2, POOLS, PAGE, KEY_HEADS * HEAD_WIDTH), 1.0, 6.0, ((1, 4), (3, 4)))
    row_page_table = touch_ends(jax.random.randint(part_keys[8], (ROWS, PAGES_ROW), 0, POOL), jax.random.fold_in(part_keys[8], 1), 0, POOL - 1).astype(jnp.int32)
    context_length = draw_context_length(jax.random.fold_in(jax.random.fold_in(arg_keys[12], part), 71), part)
    relocated_rows = draw_relocated_rows(jax.random.fold_in(jax.random.fold_in(arg_keys[12], part), 71), part)
    relocated_destination_keys = jax.random.split(jax.random.fold_in(part_keys[11], 1), MIGS // MIG_DEV)
    relocated_destination_turns = jax.random.permutation(jax.random.fold_in(part_keys[11], 3), MIGS // MIG_DEV)
    relocated_destination = jax.vmap(lambda own, number: shared_out(jax.random.fold_in(part_keys[11], 2), own, number, MIG_DEV, N_STORE, 1, MIG_CAP, 1))(relocated_destination_keys, relocated_destination_turns).reshape((MIGS, 1))
    return dict(hidden=hidden, queries=queries, fresh_rotated_keys=fresh_rotated_keys, value_matrix=value_matrix, adapter_down_factors=adapter_down_factors, adapter_up_factors=adapter_up_factors, adapter_index_rows=adapter_index_rows, key_value_pool=key_value_pool, row_page_table=row_page_table, context_length=context_length, relocated_rows=relocated_rows, relocated_destination=relocated_destination)


adapter_scale = 2.0
masked_score = -1e+30

def reference(hidden, queries, fresh_rotated_keys, value_matrix, adapter_down_factors, adapter_up_factors, adapter_index_rows, key_value_pool, row_page_table, context_length, relocated_rows, relocated_destination):
    row_total = hidden.shape[0]
    step_total = hidden.shape[1]
    token_inputs = hidden.reshape(row_total * step_total, MODEL_WIDTH)
    value_base = jnp.dot(token_inputs, value_matrix, preferred_element_type=jnp.float32)
    token_indices = jnp.repeat(adapter_index_rows[:, 0], step_total)
    token_block = 32

    def adapter_block(output_pieces):
        block_input, block_number = output_pieces
        down_factor = adapter_down_factors[block_number].astype(jnp.float32)
        up_factor = adapter_up_factors[block_number].astype(jnp.float32)
        adapter_middle = jnp.einsum('bj,bjw->bw', block_input.astype(jnp.float32), down_factor, precision=lax.Precision.HIGHEST)
        return jnp.einsum('jd,jdq->jq', adapter_middle, up_factor, precision=lax.Precision.HIGHEST)
    adapter_delta = lax.map(adapter_block, (token_inputs.reshape(-1, token_block, MODEL_WIDTH), token_indices.reshape(-1, token_block)))
    adapter_delta = adapter_delta.reshape(row_total * step_total, KEY_HEADS * HEAD_WIDTH)
    fresh_values = (value_base + adapter_scale * adapter_delta).astype(jnp.bfloat16).reshape(row_total, step_total, KEY_HEADS * HEAD_WIDTH)
    home_dev = jnp.arange(row_total, dtype=jnp.int32) // ROW_DEV
    moved_global = jnp.arange(MIGS, dtype=jnp.int32) // MIG_DEV * ROW_DEV + relocated_rows
    holder = home_dev.at[moved_global].set(relocated_destination[:, 0])
    pools = key_value_pool.reshape(2, N_STORE, POOL, PAGE, KEY_HEADS * HEAD_WIDTH)
    group = HQ // KEY_HEADS
    scale = 1.0 / math.sqrt(HEAD_WIDTH)
    span = PAGES_ROW * PAGE
    row_blk = 8

    def attend(output_pieces):
        q_blk, kn_blk, vn_blk, t_blk, l_blk, h_blk = output_pieces
        own_pools = pools[:, h_blk]
        cache_keys = jax.vmap(lambda one_pool, one_table: one_pool[one_table])(own_pools[0], t_blk)
        cache_values = jax.vmap(lambda one_pool, one_table: one_pool[one_table])(own_pools[1], t_blk)
        cache_keys = cache_keys.astype(jnp.float32).reshape(row_blk, span, KEY_HEADS, HEAD_WIDTH)
        cache_values = cache_values.astype(jnp.float32).reshape(row_blk, span, KEY_HEADS, HEAD_WIDTH)
        query_h = q_blk.astype(jnp.float32).reshape(row_blk, step_total, KEY_HEADS, group, HEAD_WIDTH)
        s_cache = jnp.einsum('bikgd,bckd->bikgc', query_h, cache_keys, precision=lax.Precision.HIGHEST) * scale
        valid = jnp.arange(span, dtype=jnp.int32)[None, :] < l_blk[:, None]
        s_cache = jnp.where(valid[:, None, None, None, :], s_cache, masked_score)
        key_new = kn_blk.astype(jnp.float32).reshape(row_blk, step_total, KEY_HEADS, HEAD_WIDTH)
        s_new = jnp.einsum('bikgd,bjkd->bikgj', query_h, key_new, precision=lax.Precision.HIGHEST) * scale
        causal = jnp.arange(step_total)[None, :] <= jnp.arange(step_total)[:, None]
        s_new = jnp.where(causal[None, :, None, None, :], s_new, masked_score)
        scores = jnp.concatenate([s_cache, s_new], axis=-1)
        largest = lax.optimization_barrier(jnp.max(scores, axis=-1, keepdims=True))
        expo = jnp.exp(scores - largest)
        total = lax.optimization_barrier(jnp.sum(expo, axis=-1))
        weights = lax.optimization_barrier(expo.astype(jnp.bfloat16)).astype(jnp.float32)
        value_new = vn_blk.astype(jnp.float32).reshape(row_blk, step_total, KEY_HEADS, HEAD_WIDTH)
        values_all = jnp.concatenate([cache_values, value_new], axis=1)
        mixed = jnp.einsum('bikgc,bckd->bikgd', weights, values_all, precision=lax.Precision.HIGHEST)
        return (mixed / total[..., None]).reshape(row_blk, step_total, HQ * HEAD_WIDTH).astype(jnp.bfloat16)
    attention = lax.map(attend, (queries.reshape(-1, row_blk, step_total, HQ * HEAD_WIDTH), fresh_rotated_keys.reshape(-1, row_blk, step_total, KEY_HEADS * HEAD_WIDTH), fresh_values.reshape(-1, row_blk, step_total, KEY_HEADS * HEAD_WIDTH), row_page_table.reshape(-1, row_blk, PAGES_ROW), context_length.reshape(-1, row_blk), holder.reshape(-1, row_blk)))
    attention = attention.reshape(row_total, step_total, HQ * HEAD_WIDTH)
    return (attention, fresh_values)
```

```python
import functools
import math

import jax
import jax.numpy as jnp
from jax import lax
from jax.experimental import pallas as pl
from jax.experimental.pallas import tpu as pltpu
from jax.sharding import PartitionSpec as P

HEAD_WIDTH = 128

adapter_scale = 2.0
masked_score = -1e30
scale = 1.0 / math.sqrt(HEAD_WIDTH)


def position_counts(table, length, pages, page_len):
    rows, entries = table.shape
    start = lax.broadcasted_iota(jnp.int32, (rows, entries), 1) * page_len
    full = jnp.where(start + page_len <= length, 1.0, 0.0)
    part = jnp.where(start < length, 1.0, 0.0) - full
    span = pages * page_len
    lane = lax.broadcasted_iota(jnp.int32, (rows, span), 1)
    page = lane // page_len
    tail = jnp.where(lane - page * page_len < length % page_len, 1.0, 0.0)
    counts = jnp.zeros((rows, span), jnp.float32)
    for p in range(pages):
        hit = table == p
        whole = jnp.sum(jnp.where(hit, full, 0.0), axis=1, keepdims=True)
        rest = jnp.sum(jnp.where(hit, part, 0.0), axis=1, keepdims=True)
        counts = jnp.where(page == p, whole + rest * tail, counts)
    return counts


def pool_attention(q_ref, keys, values, counts, here, acc_ref, top_ref, sum_ref, group):
    heads = q_ref.shape[1] // HEAD_WIDTH
    for h in range(heads):
        cols = slice(h * HEAD_WIDTH, (h + 1) * HEAD_WIDTH)
        kv = slice(h // group * HEAD_WIDTH, (h // group + 1) * HEAD_WIDTH)
        s = lax.dot_general(
            q_ref[:, cols], keys[:, kv], (((1,), (1,)), ((), ())),
            preferred_element_type=jnp.float32,
        ) * scale
        s = jnp.where(counts > 0.0, s, masked_score)
        top = jnp.max(s, axis=1, keepdims=True)
        weight = jnp.exp(s - top) * counts
        total = jnp.sum(weight, axis=1, keepdims=True)
        mixed = jnp.dot(
            weight.astype(jnp.bfloat16), values[:, kv], preferred_element_type=jnp.float32
        )
        acc_ref[:, cols] = jnp.where(here, mixed, acc_ref[:, cols])
        top_ref[:, h : h + 1] = jnp.where(here, top, top_ref[:, h : h + 1])
        sum_ref[:, h : h + 1] = jnp.where(here, total, sum_ref[:, h : h + 1])


def add_fresh(q_ref, kn_ref, fresh, acc_ref, top_ref, sum_ref, out_ref, group):
    tokens = q_ref.shape[0]
    rows = tokens // 2
    heads = q_ref.shape[1] // HEAD_WIDTH
    second = lax.broadcasted_iota(jnp.int32, (tokens, 1), 0) >= rows
    for k in range(heads // group):
        kv = slice(k * HEAD_WIDTH, (k + 1) * HEAD_WIDTH)
        key_new = kn_ref[:, kv].astype(jnp.float32)
        k0 = jnp.concatenate([key_new[:rows], key_new[:rows]], axis=0)
        k1 = jnp.concatenate([key_new[rows:], key_new[rows:]], axis=0)
        v_new = fresh[:, kv].astype(jnp.float32)
        v0 = jnp.concatenate([v_new[:rows], v_new[:rows]], axis=0)
        v1 = jnp.concatenate([v_new[rows:], v_new[rows:]], axis=0)
        for h in range(k * group, (k + 1) * group):
            cols = slice(h * HEAD_WIDTH, (h + 1) * HEAD_WIDTH)
            q = q_ref[:, cols].astype(jnp.float32)
            s0 = jnp.sum(q * k0, axis=1, keepdims=True) * scale
            s1 = jnp.sum(q * k1, axis=1, keepdims=True) * scale
            s1 = jnp.where(second, s1, masked_score)
            top = top_ref[:, h : h + 1]
            largest = jnp.maximum(top, jnp.maximum(s0, s1))
            keep = jnp.exp(top - largest)
            e0 = jnp.exp(s0 - largest)
            e1 = jnp.exp(s1 - largest)
            total = sum_ref[:, h : h + 1] * keep + e0 + e1
            mixed = acc_ref[:, cols] * keep
            mixed = mixed + e0.astype(jnp.bfloat16).astype(jnp.float32) * v0
            mixed = mixed + e1.astype(jnp.bfloat16).astype(jnp.float32) * v1
            out_ref[:, cols] = (mixed / total).astype(jnp.bfloat16)


def attention_kernel(
    stores, pages, page_len, group,
    q_ref, kn_ref, fresh_ref, table_ref, length_ref, holder_ref, pool_ref, out_ref,
    acc_ref, top_ref, sum_ref,
):
    counts = position_counts(table_ref[...], length_ref[...], pages, page_len)
    counts = jnp.concatenate([counts, counts], axis=0)
    holder = jnp.concatenate([holder_ref[...], holder_ref[...]], axis=0)
    acc_ref[...] = jnp.zeros_like(acc_ref)
    top_ref[...] = jnp.zeros_like(top_ref)
    sum_ref[...] = jnp.zeros_like(sum_ref)

    def step(s, carry):
        here = holder == s
        pool_attention(
            q_ref, pool_ref[s, 0], pool_ref[s, 1], jnp.where(here, counts, 0.0), here,
            acc_ref, top_ref, sum_ref, group,
        )
        return carry

    lax.fori_loop(0, stores, step, 0)
    add_fresh(q_ref, kn_ref, fresh_ref[...], acc_ref, top_ref, sum_ref, out_ref, group)


def per_device(
    hidden,
    queries,
    fresh_rotated_keys,
    value_matrix,
    adapter_down_factors,
    adapter_up_factors,
    adapter_index_rows,
    key_value_pool,
    row_page_table,
    context_length,
    relocated_rows,
    relocated_destination,
):
    stores = lax.axis_size("store")
    me = lax.axis_index("store")
    rows, steps, feats = hidden.shape
    tokens = rows * steps
    width = fresh_rotated_keys.shape[2]
    q_width = queries.shape[2]
    group = q_width // width
    pages, page_len = key_value_pool.shape[1:3]
    span = pages * page_len
    rank = adapter_up_factors.shape[1]
    adapters = adapter_down_factors.shape[0] * stores

    down = lax.all_gather(adapter_down_factors, "store", axis=0, tiled=True)
    up = lax.all_gather(adapter_up_factors, "store", axis=0, tiled=True)
    pool = lax.all_gather(key_value_pool.reshape(2, span, width), "store", axis=0)

    x = hidden.transpose(1, 0, 2).reshape(tokens, feats)
    q = queries.transpose(1, 0, 2).reshape(tokens, q_width)
    kn = fresh_rotated_keys.transpose(1, 0, 2).reshape(tokens, width)
    base = jnp.dot(x, value_matrix, preferred_element_type=jnp.float32)
    base = lax.psum_scatter(
        base.astype(jnp.bfloat16), "tp", scatter_dimension=1, tiled=True
    ).astype(jnp.float32)
    named = jnp.concatenate([adapter_index_rows, adapter_index_rows], axis=0)
    chosen = named == jnp.arange(adapters, dtype=jnp.int32)[None, :]
    middle = jnp.einsum("tf,afb->tab", x, down, preferred_element_type=jnp.float32)
    middle = jnp.sum(jnp.where(chosen[:, :, None], middle, 0.0), axis=1)
    middle = lax.psum(middle.astype(jnp.bfloat16), "tp")
    spread = jnp.where(chosen[:, :, None], middle[:, None, :], 0).reshape(tokens, adapters * rank)
    term = jnp.dot(
        spread, up.reshape(adapters * rank, width), preferred_element_type=jnp.float32
    )
    fresh = (base + adapter_scale * term).astype(jnp.bfloat16)

    hits = relocated_rows[None, :] == jnp.arange(rows, dtype=jnp.int32)[:, None]
    away = jnp.sum(jnp.where(hits, relocated_destination[:, 0][None, :] - me, 0), axis=1)
    holder = (me + away)[:, None]

    attention = pl.pallas_call(
        functools.partial(attention_kernel, stores, pages, page_len, group),
        out_shape=jax.ShapeDtypeStruct((tokens, q_width), jnp.bfloat16),
        in_specs=[pl.BlockSpec(memory_space=pltpu.VMEM)] * 7,
        out_specs=pl.BlockSpec(memory_space=pltpu.VMEM),
        scratch_shapes=[
            pltpu.VMEM((tokens, q_width), jnp.float32),
            pltpu.VMEM((tokens, q_width // HEAD_WIDTH), jnp.float32),
            pltpu.VMEM((tokens, q_width // HEAD_WIDTH), jnp.float32),
        ],
        compiler_params=pltpu.CompilerParams(vmem_limit_bytes=48 * 1024 * 1024),
    )(q, kn, fresh, row_page_table, context_length[:, None], holder, pool)
    return (
        attention.reshape(steps, rows, q_width).transpose(1, 0, 2),
        fresh.reshape(steps, rows, width).transpose(1, 0, 2),
    )


def solution(mesh):
    placed = (
        P(("grp", "store"), None, "tp"),
        P(("grp", "store"), None, "tp"),
        P(("grp", "store"), None, "tp"),
        P("tp", None),
        P("store", "tp", None),
        P("store", None, "tp"),
        P(("grp", "store"), None),
        P(None, ("grp", "store"), None, "tp"),
        P(("grp", "store"), None),
        P(("grp", "store")),
        P(("grp", "store")),
        P(("grp", "store"), None),
    )
    return jax.shard_map(
        per_device,
        mesh=mesh,
        in_specs=placed,
        out_specs=(P(("grp", "store"), None, "tp"), P(("grp", "store"), None, "tp")),
        check_vma=False,
    )
```

```python
import functools
import math

import jax
import jax.numpy as jnp
from jax import lax
from jax.experimental import pallas as pl
from jax.experimental.pallas import tpu as pltpu
from jax.sharding import PartitionSpec as P

HEAD_WIDTH = 128

adapter_scale = 2.0
masked_score = -1e30
scale = 1.0 / math.sqrt(HEAD_WIDTH)


def position_counts(table, length, pages, page_len):
    rows, entries = table.shape
    start = lax.broadcasted_iota(jnp.int32, (rows, entries), 1) * page_len
    full = jnp.where(start + page_len <= length, 1.0, 0.0)
    part = jnp.where(start < length, 1.0, 0.0) - full
    span = pages * page_len
    lane = lax.broadcasted_iota(jnp.int32, (rows, span), 1)
    page = lane // page_len
    tail = jnp.where(lane - page * page_len < length % page_len, 1.0, 0.0)
    counts = jnp.zeros((rows, span), jnp.float32)
    for p in range(pages):
        hit = table == p
        whole = jnp.sum(jnp.where(hit, full, 0.0), axis=1, keepdims=True)
        rest = jnp.sum(jnp.where(hit, part, 0.0), axis=1, keepdims=True)
        counts = jnp.where(page == p, whole + rest * tail, counts)
    return counts


def pool_attention(q_ref, keys, values, counts, here, acc_ref, top_ref, sum_ref, group):
    heads = q_ref.shape[1] // HEAD_WIDTH
    for h in range(heads):
        cols = slice(h * HEAD_WIDTH, (h + 1) * HEAD_WIDTH)
        kv = slice(h // group * HEAD_WIDTH, (h // group + 1) * HEAD_WIDTH)
        s = lax.dot_general(
            q_ref[:, cols], keys[:, kv], (((1,), (1,)), ((), ())),
            preferred_element_type=jnp.float32,
        ) * scale
        s = jnp.where(counts > 0.0, s, masked_score)
        top = jnp.max(s, axis=1, keepdims=True)
        weight = jnp.exp(s - top) * counts
        total = jnp.sum(weight, axis=1, keepdims=True)
        mixed = jnp.dot(
            weight.astype(jnp.bfloat16), values[:, kv], preferred_element_type=jnp.float32
        )
        acc_ref[:, cols] = jnp.where(here, mixed, acc_ref[:, cols])
        top_ref[:, h : h + 1] = jnp.where(here, top, top_ref[:, h : h + 1])
        sum_ref[:, h : h + 1] = jnp.where(here, total, sum_ref[:, h : h + 1])


def add_fresh(q_ref, kn_ref, fresh, acc_ref, top_ref, sum_ref, out_ref, group):
    tokens = q_ref.shape[0]
    rows = tokens // 2
    heads = q_ref.shape[1] // HEAD_WIDTH
    second = lax.broadcasted_iota(jnp.int32, (tokens, 1), 0) >= rows
    for k in range(heads // group):
        kv = slice(k * HEAD_WIDTH, (k + 1) * HEAD_WIDTH)
        key_new = kn_ref[:, kv].astype(jnp.float32)
        k0 = jnp.concatenate([key_new[:rows], key_new[:rows]], axis=0)
        k1 = jnp.concatenate([key_new[rows:], key_new[rows:]], axis=0)
        v_new = fresh[:, kv].astype(jnp.float32)
        v0 = jnp.concatenate([v_new[:rows], v_new[:rows]], axis=0)
        v1 = jnp.concatenate([v_new[rows:], v_new[rows:]], axis=0)
        for h in range(k * group, (k + 1) * group):
            cols = slice(h * HEAD_WIDTH, (h + 1) * HEAD_WIDTH)
            q = q_ref[:, cols].astype(jnp.float32)
            s0 = jnp.sum(q * k0, axis=1, keepdims=True) * scale
            s1 = jnp.sum(q * k1, axis=1, keepdims=True) * scale
            s1 = jnp.where(second, s1, masked_score)
            top = top_ref[:, h : h + 1]
            largest = jnp.maximum(top, jnp.maximum(s0, s1))
            keep = jnp.exp(top - largest)
            e0 = jnp.exp(s0 - largest)
            e1 = jnp.exp(s1 - largest)
            total = sum_ref[:, h : h + 1] * keep + e0 + e1
            mixed = acc_ref[:, cols] * keep
            mixed = mixed + e0.astype(jnp.bfloat16).astype(jnp.float32) * v0
            mixed = mixed + e1.astype(jnp.bfloat16).astype(jnp.float32) * v1
            out_ref[:, cols] = (mixed / total).astype(jnp.bfloat16)


def serving_kernel(
    stores, parts, pages, page_len, group,
    x_ref, q_ref, kn_ref, table_ref, length_ref, holder_ref, named_ref,
    value_hbm, down_hbm, up_hbm, pool_hbm,
    out_ref, fresh_ref,
    value_ref, down_ref, up_ref, pool_ref, base_send, base_recv, mid_send, mid_recv,
    acc_ref, top_ref, sum_ref, count_ref,
    local_sem, line_send, line_recv, pair_send, pair_recv, base_ssem, base_rsem,
    mid_ssem, mid_rsem,
):
    me = lax.axis_index("store")
    half = lax.axis_index("grp")
    tp = lax.axis_index("tp")
    tokens = x_ref.shape[0]
    width = kn_ref.shape[1]
    resident = down_ref.shape[1] * down_ref.shape[2]
    mesh_ids = pl.DeviceIdType.MESH

    loads = [
        pltpu.make_async_copy(down_hbm, down_ref.at[me], local_sem.at[0]),
        pltpu.make_async_copy(up_hbm, up_ref.at[me], local_sem.at[1]),
        pltpu.make_async_copy(pool_hbm, pool_ref.at[me], local_sem.at[2]),
        pltpu.make_async_copy(value_hbm, value_ref, local_sem.at[3]),
    ]
    for load in loads:
        load.start()

    barrier = pltpu.get_barrier_semaphore()
    for d in range(1, parts):
        pl.semaphore_signal(
            barrier, inc=1, device_id={"tp": lax.rem(tp + d, parts)}, device_id_type=mesh_ids
        )
    pl.semaphore_signal(barrier, inc=1, device_id={"grp": 1 - half}, device_id_type=mesh_ids)

    @pl.when(me > 0)
    def _():
        pl.semaphore_signal(barrier, inc=1, device_id={"store": me - 1}, device_id_type=mesh_ids)

    @pl.when(me < stores - 1)
    def _():
        pl.semaphore_signal(barrier, inc=1, device_id={"store": me + 1}, device_id_type=mesh_ids)

    ends = jnp.where(me > 0, 1, 0) + jnp.where(me < stores - 1, 1, 0)
    pl.semaphore_wait(barrier, parts + ends)

    for load in loads[:3]:
        load.wait()

    def line(stream, slot, way, t, to):
        ref = (down_ref.at[slot, half], up_ref.at[slot, half], pool_ref.at[slot])[stream]
        return pltpu.make_async_remote_copy(
            src_ref=ref, dst_ref=ref,
            send_sem=line_send.at[stream, way, t], recv_sem=line_recv.at[stream, slot],
            device_id={"store": to}, device_id_type=mesh_ids,
        )

    def pair(stream, slot, which):
        ref = (down_ref, up_ref)[stream].at[slot, which]
        return pltpu.make_async_remote_copy(
            src_ref=ref, dst_ref=ref,
            send_sem=pair_send.at[stream, slot], recv_sem=pair_recv.at[stream, slot],
            device_id={"grp": 1 - half}, device_id_type=mesh_ids,
        )

    def sends(t, act):
        @pl.when((me - t >= 0) & (me < stores - 1))
        def _():
            for stream in range(3):
                act(line(stream, me - t, 0, t, me + 1))

        @pl.when((me + t < stores) & (me > 0))
        def _():
            for stream in range(3):
                act(line(stream, me + t, 1, t, me - 1))

    def arrivals(t, streams, swap):
        @pl.when(me - 1 - t >= 0)
        def _():
            for stream in streams:
                line(stream, me - 1 - t, 0, t, me - 1).wait_recv()
                if swap:
                    pair(stream, me - 1 - t, half).start()

        @pl.when(me + 1 + t < stores)
        def _():
            for stream in streams:
                line(stream, me + 1 + t, 1, t, me + 1).wait_recv()
                if swap:
                    pair(stream, me + 1 + t, half).start()

    def attend(slot):
        holder = jnp.concatenate([holder_ref[...], holder_ref[...]], axis=0)
        here = holder == slot
        pool_attention(
            q_ref, pool_ref[slot, 0], pool_ref[slot, 1], jnp.where(here, count_ref[...], 0.0),
            here, acc_ref, top_ref, sum_ref, group,
        )

    def attend_pair(t):
        @pl.when(me - t >= 0)
        def _():
            attend(me - t)

        @pl.when(me + t < stores)
        def _():
            attend(me + t)

    sends(0, lambda copy: copy.start())

    loads[3].wait()
    for c in range(parts):
        base_send[c] = jnp.dot(
            x_ref[...], value_ref[:, c * width : (c + 1) * width],
            preferred_element_type=jnp.float32,
        ).astype(jnp.bfloat16)

    def base_copy(d):
        to = lax.rem(tp + d, parts)
        return pltpu.make_async_remote_copy(
            src_ref=base_send.at[to], dst_ref=base_recv.at[d - 1],
            send_sem=base_ssem.at[d - 1], recv_sem=base_rsem.at[d - 1],
            device_id={"tp": to}, device_id_type=mesh_ids,
        )

    def mid_copy(d):
        return pltpu.make_async_remote_copy(
            src_ref=mid_send, dst_ref=mid_recv.at[d - 1],
            send_sem=mid_ssem.at[d - 1], recv_sem=mid_rsem.at[d - 1],
            device_id={"tp": lax.rem(tp + d, parts)}, device_id_type=mesh_ids,
        )

    for d in range(1, parts):
        base_copy(d).start()

    counts = position_counts(table_ref[...], length_ref[...], pages, page_len)
    count_ref[...] = jnp.concatenate([counts, counts], axis=0)
    acc_ref[...] = jnp.zeros_like(acc_ref)
    top_ref[...] = jnp.zeros_like(top_ref)
    sum_ref[...] = jnp.zeros_like(sum_ref)
    attend(me)
    arrivals(0, (0, 1), True)
    arrivals(0, (2,), False)

    def step(t, carry):
        sends(t, lambda copy: copy.start())
        attend_pair(t)
        arrivals(t, (0, 1), True)

        @pl.when(t < stores - 2)
        def _():
            arrivals(t, (2,), False)

        return carry

    lax.fori_loop(1, stores - 1, step, 0)

    named = jnp.concatenate([named_ref[...], named_ref[...]], axis=0)
    lane = lax.broadcasted_iota(jnp.int32, (tokens, resident), 1)
    own_lane = lane // (resident // 2)

    def middle(k, total):
        @pl.when(k != me)
        def _():
            for stream in range(2):
                pair(stream, k, 1 - half).wait_recv()

        product = lax.dot_general(
            x_ref[...], down_ref[k].reshape(resident, down_ref.shape[3]),
            (((1,), (1,)), ((), ())), preferred_element_type=jnp.float32,
        )
        return total + jnp.where(named == own_lane + 2 * k, product, 0.0)

    mid = lax.fori_loop(0, stores, middle, jnp.zeros((tokens, resident), jnp.float32))
    mid_send[...] = mid.astype(jnp.bfloat16)
    for d in range(1, parts):
        mid_copy(d).start()

    arrivals(stores - 2, (2,), False)
    attend_pair(stores - 1)

    for d in range(1, parts):
        base_copy(d).wait()
        mid_copy(d).wait()
    base = base_send[tp].astype(jnp.float32)
    mid = mid_send[...].astype(jnp.float32)
    for d in range(1, parts):
        base = base + base_recv[d - 1].astype(jnp.float32)
        mid = mid + mid_recv[d - 1].astype(jnp.float32)

    def upward(k, total):
        chosen = jnp.where(named // 2 == k, mid, 0.0).astype(jnp.bfloat16)
        return total + jnp.dot(
            chosen, up_ref[k].reshape(resident, width), preferred_element_type=jnp.float32
        )

    term = lax.fori_loop(0, stores, upward, jnp.zeros((tokens, width), jnp.float32))
    fresh = (base + adapter_scale * term).astype(jnp.bfloat16)
    fresh_ref[...] = fresh
    add_fresh(q_ref, kn_ref, fresh, acc_ref, top_ref, sum_ref, out_ref, group)

    def finish(t, carry):
        sends(t, lambda copy: copy.wait_send())
        return carry

    lax.fori_loop(0, stores - 1, finish, 0)

    def finish_pair(k, carry):
        @pl.when(k != me)
        def _():
            for stream in range(2):
                pair(stream, k, half).wait_send()

        return carry

    lax.fori_loop(0, stores, finish_pair, 0)


def per_device(
    hidden,
    queries,
    fresh_rotated_keys,
    value_matrix,
    adapter_down_factors,
    adapter_up_factors,
    adapter_index_rows,
    key_value_pool,
    row_page_table,
    context_length,
    relocated_rows,
    relocated_destination,
):
    stores = lax.axis_size("store")
    me = lax.axis_index("store")
    rows, steps, feats = hidden.shape
    tokens = rows * steps
    width = fresh_rotated_keys.shape[2]
    q_width = queries.shape[2]
    group = q_width // width
    pages, page_len = key_value_pool.shape[1:3]
    span = pages * page_len
    parts = lax.axis_size("tp")
    resident = adapter_up_factors.shape[0] * adapter_up_factors.shape[1]

    x = hidden.transpose(1, 0, 2).reshape(tokens, feats)
    q = queries.transpose(1, 0, 2).reshape(tokens, q_width)
    kn = fresh_rotated_keys.transpose(1, 0, 2).reshape(tokens, width)
    down = adapter_down_factors.transpose(0, 2, 1).reshape(2, resident // 2, feats)
    up = adapter_up_factors.reshape(2, resident // 2, width)
    pool = key_value_pool.reshape(2, span, width)

    hits = relocated_rows[None, :] == jnp.arange(rows, dtype=jnp.int32)[:, None]
    away = jnp.sum(jnp.where(hits, relocated_destination[:, 0][None, :] - me, 0), axis=1)
    holder = (me + away)[:, None]

    heads = q_width // HEAD_WIDTH
    dma = pltpu.SemaphoreType.DMA
    attention, fresh = pl.pallas_call(
        functools.partial(serving_kernel, stores, parts, pages, page_len, group),
        out_shape=(
            jax.ShapeDtypeStruct((tokens, q_width), jnp.bfloat16),
            jax.ShapeDtypeStruct((tokens, width), jnp.bfloat16),
        ),
        in_specs=[pl.BlockSpec(memory_space=pltpu.VMEM)] * 7
        + [pl.BlockSpec(memory_space=pl.ANY)] * 4,
        out_specs=[pl.BlockSpec(memory_space=pltpu.VMEM)] * 2,
        scratch_shapes=[
            pltpu.VMEM(value_matrix.shape, jnp.bfloat16),
            pltpu.VMEM((stores,) + down.shape, jnp.bfloat16),
            pltpu.VMEM((stores,) + up.shape, jnp.bfloat16),
            pltpu.VMEM((stores,) + pool.shape, jnp.bfloat16),
            pltpu.VMEM((parts, tokens, width), jnp.bfloat16),
            pltpu.VMEM((parts - 1, tokens, width), jnp.bfloat16),
            pltpu.VMEM((tokens, resident), jnp.bfloat16),
            pltpu.VMEM((parts - 1, tokens, resident), jnp.bfloat16),
            pltpu.VMEM((tokens, q_width), jnp.float32),
            pltpu.VMEM((tokens, heads), jnp.float32),
            pltpu.VMEM((tokens, heads), jnp.float32),
            pltpu.VMEM((tokens, span), jnp.float32),
            dma((4,)),
            dma((3, 2, stores)),
            dma((3, stores)),
            dma((2, stores)),
            dma((2, stores)),
            dma((parts - 1,)),
            dma((parts - 1,)),
            dma((parts - 1,)),
            dma((parts - 1,)),
        ],
        compiler_params=pltpu.CompilerParams(
            collective_id=0, has_side_effects=True, vmem_limit_bytes=48 * 1024 * 1024
        ),
    )(
        x, q, kn, row_page_table, context_length[:, None], holder, adapter_index_rows,
        value_matrix, down, up, pool,
    )
    return (
        attention.reshape(steps, rows, q_width).transpose(1, 0, 2),
        fresh.reshape(steps, rows, width).transpose(1, 0, 2),
    )


def solution(mesh):
    placed = (
        P(("grp", "store"), None, "tp"),
        P(("grp", "store"), None, "tp"),
        P(("grp", "store"), None, "tp"),
        P("tp", None),
        P("store", "tp", None),
        P("store", None, "tp"),
        P(("grp", "store"), None),
        P(None, ("grp", "store"), None, "tp"),
        P(("grp", "store"), None),
        P(("grp", "store")),
        P(("grp", "store")),
        P(("grp", "store"), None),
    )
    return jax.shard_map(
        per_device,
        mesh=mesh,
        in_specs=placed,
        out_specs=(P(("grp", "store"), None, "tp"), P(("grp", "store"), None, "tp")),
        check_vma=False,
    )
```

```python
import functools
import math

import jax
import jax.numpy as jnp
from jax import lax
from jax.experimental import pallas as pl
from jax.experimental.pallas import tpu as pltpu
from jax.sharding import PartitionSpec as P

HEAD_WIDTH = 128

adapter_scale = 2.0
masked_score = -1e30
scale = 1.0 / math.sqrt(HEAD_WIDTH)


def position_counts(table, length, pages, page_len):
    rows, entries = table.shape
    start = lax.broadcasted_iota(jnp.int32, (rows, entries), 1) * page_len
    full = jnp.where(start + page_len <= length, 1.0, 0.0)
    part = jnp.where(start < length, 1.0, 0.0) - full
    span = pages * page_len
    lane = lax.broadcasted_iota(jnp.int32, (rows, span), 1)
    page = lane // page_len
    tail = jnp.where(lane - page * page_len < length % page_len, 1.0, 0.0)
    counts = jnp.zeros((rows, span), jnp.float32)
    for p in range(pages):
        hit = table == p
        whole = jnp.sum(jnp.where(hit, full, 0.0), axis=1, keepdims=True)
        rest = jnp.sum(jnp.where(hit, part, 0.0), axis=1, keepdims=True)
        counts = jnp.where(page == p, whole + rest * tail, counts)
    return counts


def pool_attention(q_ref, keys, values, counts, here, acc_ref, top_ref, sum_ref, group):
    heads = q_ref.shape[1] // HEAD_WIDTH
    for h in range(heads):
        cols = slice(h * HEAD_WIDTH, (h + 1) * HEAD_WIDTH)
        kv = slice(h // group * HEAD_WIDTH, (h // group + 1) * HEAD_WIDTH)
        s = lax.dot_general(
            q_ref[:, cols], keys[:, kv], (((1,), (1,)), ((), ())),
            preferred_element_type=jnp.float32,
        ) * scale
        s = jnp.where(counts > 0.0, s, masked_score)
        top = jnp.max(s, axis=1, keepdims=True)
        weight = jnp.exp(s - top) * counts
        total = jnp.sum(weight, axis=1, keepdims=True)
        mixed = jnp.dot(
            weight.astype(jnp.bfloat16), values[:, kv], preferred_element_type=jnp.float32
        )
        acc_ref[:, cols] = jnp.where(here, mixed, acc_ref[:, cols])
        top_ref[:, h : h + 1] = jnp.where(here, top, top_ref[:, h : h + 1])
        sum_ref[:, h : h + 1] = jnp.where(here, total, sum_ref[:, h : h + 1])


def fresh_scores(q_ref, kn_ref, first_ref, second_ref, group):
    tokens = q_ref.shape[0]
    rows = tokens // 2
    heads = q_ref.shape[1] // HEAD_WIDTH
    second = lax.broadcasted_iota(jnp.int32, (tokens, 1), 0) >= rows
    for k in range(heads // group):
        kv = slice(k * HEAD_WIDTH, (k + 1) * HEAD_WIDTH)
        key_new = kn_ref[:, kv].astype(jnp.float32)
        k0 = jnp.concatenate([key_new[:rows], key_new[:rows]], axis=0)
        k1 = jnp.concatenate([key_new[rows:], key_new[rows:]], axis=0)
        for h in range(k * group, (k + 1) * group):
            q = q_ref[:, h * HEAD_WIDTH : (h + 1) * HEAD_WIDTH].astype(jnp.float32)
            s0 = jnp.sum(q * k0, axis=1, keepdims=True) * scale
            s1 = jnp.sum(q * k1, axis=1, keepdims=True) * scale
            first_ref[:, h : h + 1] = s0
            second_ref[:, h : h + 1] = jnp.where(second, s1, masked_score)


def add_fresh(fresh, acc_ref, top_ref, sum_ref, first_ref, second_ref, out_ref, group):
    rows = fresh.shape[0] // 2
    heads = top_ref.shape[1]
    s0, s1, top = first_ref[...], second_ref[...], top_ref[...]
    largest = jnp.maximum(top, jnp.maximum(s0, s1))
    keep = jnp.exp(top - largest)
    e0 = jnp.exp(s0 - largest)
    e1 = jnp.exp(s1 - largest)
    share = 1.0 / (sum_ref[...] * keep + e0 + e1)
    keep = keep * share
    e0 = e0.astype(jnp.bfloat16).astype(jnp.float32) * share
    e1 = e1.astype(jnp.bfloat16).astype(jnp.float32) * share
    for k in range(heads // group):
        v_new = fresh[:, k * HEAD_WIDTH : (k + 1) * HEAD_WIDTH].astype(jnp.float32)
        v0 = jnp.concatenate([v_new[:rows], v_new[:rows]], axis=0)
        v1 = jnp.concatenate([v_new[rows:], v_new[rows:]], axis=0)
        for h in range(k * group, (k + 1) * group):
            cols = slice(h * HEAD_WIDTH, (h + 1) * HEAD_WIDTH)
            one = slice(h, h + 1)
            mixed = acc_ref[:, cols] * keep[:, one] + e0[:, one] * v0 + e1[:, one] * v1
            out_ref[:, cols] = mixed.astype(jnp.bfloat16)


def as_column(row):
    count = row.shape[1]
    across = lax.broadcasted_iota(jnp.int32, (count, count), 1)
    down = lax.broadcasted_iota(jnp.int32, (count, count), 0)
    return jnp.sum(jnp.where(across == down, row, 0), axis=1, keepdims=True)


def serving_kernel(
    stores, parts, pages, page_len, group,
    x_ref, q_ref, kn_ref, table_ref, length_ref, named_ref, listed_ref, dest_ref,
    value_hbm, down_hbm, up_hbm, pool_hbm,
    out_ref, fresh_ref,
    value_ref, down_ref, up_ref, pool_ref, base_send, base_recv, mid_send, mid_recv,
    acc_ref, top_ref, sum_ref, count_ref, first_ref, second_ref, holder_ref,
    local_sem, line_send, line_recv, pair_send, pair_recv, base_ssem, base_rsem,
    mid_ssem, mid_rsem,
):
    me = lax.axis_index("store")
    half = lax.axis_index("grp")
    tp = lax.axis_index("tp")
    tokens = x_ref.shape[0]
    width = kn_ref.shape[1]
    resident = down_ref.shape[1] * down_ref.shape[2]
    mesh_ids = pl.DeviceIdType.MESH

    loads = [
        pltpu.make_async_copy(down_hbm, down_ref.at[me], local_sem.at[0]),
        pltpu.make_async_copy(up_hbm, up_ref.at[me], local_sem.at[1]),
        pltpu.make_async_copy(pool_hbm, pool_ref.at[me], local_sem.at[2]),
        pltpu.make_async_copy(value_hbm, value_ref, local_sem.at[3]),
    ]
    for load in loads:
        load.start()

    barrier = pltpu.get_barrier_semaphore()
    for d in range(1, parts):
        pl.semaphore_signal(
            barrier, inc=1, device_id={"tp": lax.rem(tp + d, parts)}, device_id_type=mesh_ids
        )
    pl.semaphore_signal(barrier, inc=1, device_id={"grp": 1 - half}, device_id_type=mesh_ids)

    @pl.when(me > 0)
    def _():
        pl.semaphore_signal(barrier, inc=1, device_id={"store": me - 1}, device_id_type=mesh_ids)

    @pl.when(me < stores - 1)
    def _():
        pl.semaphore_signal(barrier, inc=1, device_id={"store": me + 1}, device_id_type=mesh_ids)

    ends = jnp.where(me > 0, 1, 0) + jnp.where(me < stores - 1, 1, 0)
    pl.semaphore_wait(barrier, parts + ends)

    for load in loads[:3]:
        load.wait()

    def line(stream, slot, way, t, to):
        ref = (down_ref.at[slot, half], up_ref.at[slot, half], pool_ref.at[slot])[stream]
        return pltpu.make_async_remote_copy(
            src_ref=ref, dst_ref=ref,
            send_sem=line_send.at[stream, way, t], recv_sem=line_recv.at[stream, slot],
            device_id={"store": to}, device_id_type=mesh_ids,
        )

    def pair(stream, slot, which):
        ref = (down_ref, up_ref)[stream].at[slot, which]
        return pltpu.make_async_remote_copy(
            src_ref=ref, dst_ref=ref,
            send_sem=pair_send.at[stream, slot], recv_sem=pair_recv.at[stream, slot],
            device_id={"grp": 1 - half}, device_id_type=mesh_ids,
        )

    def sends(t, act):
        @pl.when((me - t >= 0) & (me < stores - 1))
        def _():
            for stream in range(3):
                act(line(stream, me - t, 0, t, me + 1))

        @pl.when((me + t < stores) & (me > 0))
        def _():
            for stream in range(3):
                act(line(stream, me + t, 1, t, me - 1))

    def arrivals(t, streams, swap):
        @pl.when(me - 1 - t >= 0)
        def _():
            for stream in streams:
                line(stream, me - 1 - t, 0, t, me - 1).wait_recv()
                if swap:
                    pair(stream, me - 1 - t, half).start()

        @pl.when(me + 1 + t < stores)
        def _():
            for stream in streams:
                line(stream, me + 1 + t, 1, t, me + 1).wait_recv()
                if swap:
                    pair(stream, me + 1 + t, half).start()

    def attend(slot):
        here = holder_ref[...] == slot
        pool_attention(
            q_ref, pool_ref[slot, 0], pool_ref[slot, 1], jnp.where(here, count_ref[...], 0.0),
            here, acc_ref, top_ref, sum_ref, group,
        )

    def attend_pair(t):
        @pl.when(me - t >= 0)
        def _():
            attend(me - t)

        @pl.when(me + t < stores)
        def _():
            attend(me + t)

    sends(0, lambda copy: copy.start())

    loads[3].wait()
    for c in range(parts):
        base_send[c] = jnp.dot(
            x_ref[...], value_ref[:, c * width : (c + 1) * width],
            preferred_element_type=jnp.float32,
        ).astype(jnp.bfloat16)

    def base_copy(d):
        to = lax.rem(tp + d, parts)
        return pltpu.make_async_remote_copy(
            src_ref=base_send.at[to], dst_ref=base_recv.at[d - 1],
            send_sem=base_ssem.at[d - 1], recv_sem=base_rsem.at[d - 1],
            device_id={"tp": to}, device_id_type=mesh_ids,
        )

    def mid_copy(d):
        return pltpu.make_async_remote_copy(
            src_ref=mid_send, dst_ref=mid_recv.at[d - 1],
            send_sem=mid_ssem.at[d - 1], recv_sem=mid_rsem.at[d - 1],
            device_id={"tp": lax.rem(tp + d, parts)}, device_id_type=mesh_ids,
        )

    for d in range(1, parts):
        base_copy(d).start()

    rows = tokens // 2
    hits = listed_ref[...] == lax.broadcasted_iota(
        jnp.int32, (rows, listed_ref.shape[1]), 0
    )
    holder = me + jnp.sum(jnp.where(hits, dest_ref[...] - me, 0), axis=1, keepdims=True)
    holder_ref[...] = jnp.concatenate([holder, holder], axis=0)
    counts = position_counts(table_ref[...], as_column(length_ref[...]), pages, page_len)
    count_ref[...] = jnp.concatenate([counts, counts], axis=0)
    acc_ref[...] = jnp.zeros_like(acc_ref)
    top_ref[...] = jnp.zeros_like(top_ref)
    sum_ref[...] = jnp.zeros_like(sum_ref)
    attend(me)
    fresh_scores(q_ref, kn_ref, first_ref, second_ref, group)
    arrivals(0, (0, 1), True)
    arrivals(0, (2,), False)

    def step(t, carry):
        sends(t, lambda copy: copy.start())
        attend_pair(t)
        arrivals(t, (0, 1), True)

        @pl.when(t < stores - 2)
        def _():
            arrivals(t, (2,), False)

        return carry

    lax.fori_loop(1, stores - 1, step, 0)

    named = as_column(named_ref[...])
    named = jnp.concatenate([named, named], axis=0)
    lane = lax.broadcasted_iota(jnp.int32, (tokens, resident), 1)
    own_lane = lane // (resident // 2)

    def middle(k, total):
        @pl.when(k != me)
        def _():
            for stream in range(2):
                pair(stream, k, 1 - half).wait_recv()

        product = lax.dot_general(
            x_ref[...], down_ref[k].reshape(resident, down_ref.shape[3]),
            (((1,), (1,)), ((), ())), preferred_element_type=jnp.float32,
        )
        return total + jnp.where(named == own_lane + 2 * k, product, 0.0)

    mid = lax.fori_loop(0, stores, middle, jnp.zeros((tokens, resident), jnp.float32))
    mid_send[...] = mid.astype(jnp.bfloat16)
    for d in range(1, parts):
        mid_copy(d).start()

    arrivals(stores - 2, (2,), False)
    attend_pair(stores - 1)

    for d in range(1, parts):
        base_copy(d).wait()
        mid_copy(d).wait()
    base = base_send[tp].astype(jnp.float32)
    mid = mid_send[...].astype(jnp.float32)
    for d in range(1, parts):
        base = base + base_recv[d - 1].astype(jnp.float32)
        mid = mid + mid_recv[d - 1].astype(jnp.float32)

    def upward(k, total):
        chosen = jnp.where(named // 2 == k, mid, 0.0).astype(jnp.bfloat16)
        return total + jnp.dot(
            chosen, up_ref[k].reshape(resident, width), preferred_element_type=jnp.float32
        )

    term = lax.fori_loop(0, stores, upward, jnp.zeros((tokens, width), jnp.float32))
    fresh = (base + adapter_scale * term).astype(jnp.bfloat16)
    fresh_ref[...] = fresh
    add_fresh(fresh, acc_ref, top_ref, sum_ref, first_ref, second_ref, out_ref, group)

    def finish(t, carry):
        sends(t, lambda copy: copy.wait_send())
        return carry

    lax.fori_loop(0, stores - 1, finish, 0)

    def finish_pair(k, carry):
        @pl.when(k != me)
        def _():
            for stream in range(2):
                pair(stream, k, half).wait_send()

        return carry

    lax.fori_loop(0, stores, finish_pair, 0)


def per_device(
    hidden,
    queries,
    fresh_rotated_keys,
    value_matrix,
    adapter_down_factors,
    adapter_up_factors,
    adapter_index_rows,
    key_value_pool,
    row_page_table,
    context_length,
    relocated_rows,
    relocated_destination,
):
    stores = lax.axis_size("store")
    rows, steps, feats = hidden.shape
    tokens = rows * steps
    width = fresh_rotated_keys.shape[2]
    q_width = queries.shape[2]
    group = q_width // width
    pages, page_len = key_value_pool.shape[1:3]
    span = pages * page_len
    parts = lax.axis_size("tp")
    resident = adapter_up_factors.shape[0] * adapter_up_factors.shape[1]

    x = hidden.transpose(1, 0, 2).reshape(tokens, feats)
    q = queries.transpose(1, 0, 2).reshape(tokens, q_width)
    kn = fresh_rotated_keys.transpose(1, 0, 2).reshape(tokens, width)
    down = adapter_down_factors.transpose(0, 2, 1).reshape(2, resident // 2, feats)
    up = adapter_up_factors.reshape(2, resident // 2, width)
    pool = key_value_pool.reshape(2, span, width)

    heads = q_width // HEAD_WIDTH
    dma = pltpu.SemaphoreType.DMA
    attention, fresh = pl.pallas_call(
        functools.partial(serving_kernel, stores, parts, pages, page_len, group),
        out_shape=(
            jax.ShapeDtypeStruct((tokens, q_width), jnp.bfloat16),
            jax.ShapeDtypeStruct((tokens, width), jnp.bfloat16),
        ),
        in_specs=[pl.BlockSpec(memory_space=pltpu.VMEM)] * 8
        + [pl.BlockSpec(memory_space=pltpu.HBM)] * 4,
        out_specs=[pl.BlockSpec(memory_space=pltpu.VMEM)] * 2,
        scratch_shapes=[
            pltpu.VMEM(value_matrix.shape, jnp.bfloat16),
            pltpu.VMEM((stores,) + down.shape, jnp.bfloat16),
            pltpu.VMEM((stores,) + up.shape, jnp.bfloat16),
            pltpu.VMEM((stores,) + pool.shape, jnp.bfloat16),
            pltpu.VMEM((parts, tokens, width), jnp.bfloat16),
            pltpu.VMEM((parts - 1, tokens, width), jnp.bfloat16),
            pltpu.VMEM((tokens, resident), jnp.bfloat16),
            pltpu.VMEM((parts - 1, tokens, resident), jnp.bfloat16),
            pltpu.VMEM((tokens, q_width), jnp.float32),
            pltpu.VMEM((tokens, heads), jnp.float32),
            pltpu.VMEM((tokens, heads), jnp.float32),
            pltpu.VMEM((tokens, span), jnp.float32),
            pltpu.VMEM((tokens, heads), jnp.float32),
            pltpu.VMEM((tokens, heads), jnp.float32),
            pltpu.VMEM((tokens, 1), jnp.int32),
            dma((4,)),
            dma((3, 2, stores)),
            dma((3, stores)),
            dma((2, stores)),
            dma((2, stores)),
            dma((parts - 1,)),
            dma((parts - 1,)),
            dma((parts - 1,)),
            dma((parts - 1,)),
        ],
        compiler_params=pltpu.CompilerParams(
            collective_id=0, has_side_effects=True, vmem_limit_bytes=62 * 1024 * 1024
        ),
    )(
        x, q, kn, row_page_table, context_length[None, :],
        adapter_index_rows.reshape(1, rows), relocated_rows[None, :],
        relocated_destination.reshape(1, relocated_rows.shape[0]),
        value_matrix, down, up, pool,
    )
    return (
        attention.reshape(steps, rows, q_width).transpose(1, 0, 2),
        fresh.reshape(steps, rows, width).transpose(1, 0, 2),
    )


def solution(mesh):
    placed = (
        P(("grp", "store"), None, "tp"),
        P(("grp", "store"), None, "tp"),
        P(("grp", "store"), None, "tp"),
        P("tp", None),
        P("store", "tp", None),
        P("store", None, "tp"),
        P(("grp", "store"), None),
        P(None, ("grp", "store"), None, "tp"),
        P(("grp", "store"), None),
        P(("grp", "store")),
        P(("grp", "store")),
        P(("grp", "store"), None),
    )
    return jax.shard_map(
        per_device,
        mesh=mesh,
        in_specs=placed,
        out_specs=(P(("grp", "store"), None, "tp"), P(("grp", "store"), None, "tp")),
        check_vma=False,
    )
```
